256 devices in a mesh: ctx: 32 (over z, x), head: 8 (over y, core).
Axes of the slice: x: 4, y: 4, z: 8, core: 2. Of those that a mesh axis runs over, the one named last changes fastest.
Arguments:
- latent_cache: bfloat16 [2048, 36864], P('ctx'), may hold values from -6 to 6
- queries: bfloat16 [4096, 24576], P('ctx', 'head'), may hold values from -320 to 320
- chosen: int32 [4096, 32], P('ctx'), may hold values from 0 to 2047, as said below
- key_up: bfloat16 [128, 128, 512], P('head'), may hold values from -0.5 to 0.5
- value_up: bfloat16 [128, 512, 128], P('head'), may hold values from -2.390625 to 2.390625
Outputs:
- attended: bfloat16 [4096, 16384], P('ctx', 'head')
The draws below stay inside these ranges and needn't reach their ends.
Inputs may be any that keep to these rules, and one draw needn't show every extreme that they name: `chosen`: A query's 32 blocks are distinct. The queries of one ctx index (aligned blocks of 128 rows) choose exactly 44 distinct blocks together; at most 3 of them lie in one ctx index's 64 cache blocks, and exactly 3 in the newest 64 blocks.
All inputs are finite; a program needn't handle non-finite values.
Results may differ from the reference program's by a relative error of at most 0.0095.
Values may be sent and summed in bfloat16 or wider, within the bound.
A program may use at most 128 MiB of HBM per device.

```python
import math
import jax
import jax.numpy as jnp
from jax import lax

LATENT = 512
ROPE = 64
NOPE = 128
VDIM = 128
HEADS = 128
BLOCK = 64
SEL = 32
POOL = 44
QD = 128
BD = 64
CAP = 3
QUERIES = 4096
BLOCKS = 2048


def chosen_table(key):
    base_key = jax.random.fold_in(key, 101)
    owner_count = BLOCKS // BD
    group_count = QUERIES // QD

    def one_group(group_key):
        keys_list = jax.random.split(group_key, 6)
        offsets = jax.vmap(lambda owner_key: jax.random.permutation(owner_key, BD)[:CAP])(jax.random.split(keys_list[0], owner_count))
        owners = jnp.arange(owner_count, dtype=jnp.int32)[:, None]
        candidates = (owners * BD + offsets).reshape(-1)
        raw_score = jax.random.randint(keys_list[1], (owner_count, CAP), 0, owner_count) + owners
        tie_break = jax.random.permutation(keys_list[2], owner_count * CAP)
        ranked = raw_score.reshape(-1) * (owner_count * CAP) + tie_break
        newest = jnp.broadcast_to(owners == owner_count - 1, (owner_count, CAP)).reshape(-1)
        ranked = jnp.where(newest, 4 * owner_count * owner_count * CAP, ranked)
        top_values, top_index = lax.top_k(ranked, POOL)
        pool_blocks = candidates[top_index][jax.random.permutation(keys_list[3], POOL)]
        cover_rows = (POOL + SEL - 1) // SEL
        query_rank = jax.random.permutation(keys_list[4], QD)[:, None]
        cover_pos = (query_rank * SEL + jnp.arange(SEL, dtype=jnp.int32)[None, :]) % POOL
        random_pos = jax.vmap(lambda query_key: jax.random.permutation(query_key, POOL)[:SEL])(jax.random.split(keys_list[5], QD))
        positions = jnp.where(query_rank < cover_rows, cover_pos, random_pos)
        return pool_blocks[positions].astype(jnp.int32)
    table = jax.vmap(one_group)(jax.random.split(base_key, group_count))
    return table.reshape(QUERIES, SEL)


def cache_table(key):
    base_key = jax.random.fold_in(key, 202)
    latent_key, rope_key = jax.random.split(base_key)
    latent_part = jax.random.truncated_normal(latent_key, -6.0, 6.0, (BLOCKS, BLOCK, LATENT), jnp.float32)
    rope_part = jax.random.truncated_normal(rope_key, -6.0, 6.0, (BLOCKS, BLOCK, ROPE), jnp.float32)
    second_row = rope_part[:, 1]
    rope_part = rope_part.at[:, 1].set(second_row)
    return jnp.concatenate([latent_part, rope_part], axis=2)


def draw_chosen(key, part):
    return chosen_table(key)


def draw_latent_cache(key, part):
    whole = cache_table(key)
    return whole.reshape(BLOCKS, BLOCK * (LATENT + ROPE)).astype(jnp.bfloat16)


def draw_queries(key, part):
    own_key = jax.random.fold_in(key, 303)
    values = jax.random.truncated_normal(own_key, -6.0, 6.0, (QUERIES, HEADS, NOPE + ROPE), jnp.float32)
    return values.reshape(QUERIES, HEADS * (NOPE + ROPE)).astype(jnp.bfloat16)


def shard_levels(key, extent, cuts, smallest, high):
    def one(axis_at, shards_of):
        steps = jax.random.uniform(jax.random.fold_in(jax.random.fold_in(key, 6), axis_at), (shards_of,), jnp.float32, smallest / len(cuts), high / len(cuts))
        return jnp.repeat(jnp.exp(steps), extent[axis_at] // shards_of).reshape((-1,) + (1,) * (len(extent) - axis_at - 1))

    gain = one(*cuts[0])
    for cut in cuts[1:]:
        gain = gain * one(*cut)
    return gain


def bell_draw(rng, shape, scale, reach, cuts=(), kind=jnp.bfloat16):
    values = jax.random.normal(rng, shape, jnp.float32) * scale
    if len(cuts) > 0:
        values = shard_levels(rng, shape, cuts, -0.22, 0.18) * values
    return jnp.clip(values, min=-reach, max=reach).astype(kind)


def setup_inputs(seed: int = 0) -> dict:
    key_of = jax.random.split(jax.random.key(seed), 6)
    latent_cache = draw_latent_cache(jax.random.fold_in(key_of[5], 71), 0)
    queries = draw_queries(jax.random.fold_in(key_of[5], 71), 0)
    chosen = draw_chosen(jax.random.fold_in(key_of[5], 71), 0)
    key_up = bell_draw(key_of[3], (HEADS, NOPE, LATENT), NOPE ** -0.5, 0.5, ((0, 8),))
    value_up = bell_draw(key_of[4], (HEADS, LATENT, VDIM), 0.4, 2.390625, ((0, 8),))
    return dict(latent_cache=latent_cache, queries=queries, chosen=chosen, key_up=key_up, value_up=value_up)


def reference(latent_cache, queries, chosen, key_up, value_up):
    row_width = LATENT + ROPE
    score_scale = (NOPE + ROPE) ** -0.5
    cache_rows = latent_cache.reshape(BLOCKS, BLOCK, row_width)
    up_keys = key_up.astype(jnp.float32)
    up_values = value_up.astype(jnp.float32)
    per_step = math.gcd(QUERIES, 8)
    steps_count = QUERIES // per_step

    def score_block(inputs):
        query_rows, picked = inputs
        heads_view = query_rows.reshape(per_step, HEADS, NOPE + ROPE)
        latent_query = jnp.einsum("qhn,hnl->qhl", heads_view[:, :, :NOPE].astype(jnp.float32), up_keys)
        latent_query = lax.optimization_barrier(latent_query.astype(jnp.bfloat16)).astype(jnp.float32)
        full_query = jnp.concatenate([latent_query, heads_view[:, :, NOPE:].astype(jnp.float32)], axis=2)
        keys_all = cache_rows[picked.astype(jnp.int32)].reshape(per_step, SEL * BLOCK, row_width).astype(jnp.float32)
        scores = jnp.einsum("qhr,qkr->qhk", full_query, keys_all) * score_scale
        largest = jnp.max(scores, axis=2, keepdims=True)
        exponent = jnp.exp(scores - largest)
        denominator = jnp.sum(exponent, axis=2)
        weights = lax.optimization_barrier(exponent.astype(jnp.bfloat16)).astype(jnp.float32)
        mixed = jnp.einsum("qhk,qkl->qhl", weights, keys_all[:, :, :LATENT]) / denominator[:, :, None]
        mixed = lax.optimization_barrier(mixed.astype(jnp.bfloat16)).astype(jnp.float32)
        result = jnp.einsum("qhl,hlv->qhv", mixed, up_values)
        return result.astype(jnp.bfloat16).reshape(per_step, HEADS * VDIM)

    stacked = lax.map(score_block, (queries.reshape(steps_count, per_step, -1), chosen.reshape(steps_count, per_step, SEL)))
    return stacked.reshape(QUERIES, HEADS * VDIM)
```

```python
import functools

import jax
import jax.numpy as jnp
from jax import lax
from jax.experimental import pallas as pl
from jax.experimental.pallas import tpu as pltpu
from jax.sharding import PartitionSpec as P

BF = jnp.bfloat16
F32 = jnp.float32
CTX = 32
HEADS = 16
ROWS = 128
BD = 64
CAP = 3
POOL = 44
SLOTS = 48
SHARE = 4608
PAIR = 1152
CHUNKS = 4
KEYS = 768
GROUPS = ((0, 2), (2, 2), (4, 2), (6, 1))
HP = 2
HIDE = -1e30
SCALE = (192**-0.5) * 1.4426950408889634


def nn(a, b):
    return lax.dot_general(a, b, (((1,), (0,)), ((), ())), preferred_element_type=F32)


def nt(a, b):
    return lax.dot_general(a, b, (((1,), (1,)), ((), ())), preferred_element_type=F32)


def iota(shape, dim):
    return lax.broadcasted_iota(jnp.int32, shape, dim)


def ones(cond):
    return jnp.where(cond, 1.0, 0.0).astype(BF)


def slot_of_row(r):
    return jnp.where(r < 5, 0, jnp.where(r < 10, 1, 2))


def kernel(
    cache_hbm, queries_hbm, chosen_hbm, kup_hbm, vup_hbm, out_ref,
    shard, qraw, picks, kup, vup, req_send, req_recv, pack_send, pack_recv,
    pool, rext, qext, acc, top, total,
    in_sem, req_sem, pack_ssem, pack_rsem, gat_ssem, gat_rsem,
):
    me = lax.axis_index("ctx")
    hd = lax.axis_index("head")
    core = lax.rem(hd, 2)
    up = lax.rem(hd + 2, 8)
    down = lax.rem(hd + 6, 8)
    mate = hd + 1 - 2 * core
    far = lax.rem(hd + 4, 8)

    loads = []
    for n, (src, dst) in enumerate(
        (
            (chosen_hbm, picks),
            (cache_hbm.at[:, pl.ds(pl.multiple_of(hd * SHARE, 128), SHARE)], shard),
            (queries_hbm, qraw),
            (kup_hbm, kup),
            (vup_hbm, vup),
        )
    ):
        load = pltpu.make_async_copy(src, dst, in_sem.at[n])
        load.start()
        loads.append(load)

    barrier = pltpu.get_barrier_semaphore()

    def greet(k, carry):
        pl.semaphore_signal(barrier, inc=1, device_id={"ctx": lax.rem(me + k, CTX)})
        return carry

    lax.fori_loop(1, CTX, greet, 0)
    for peer in (up, down, mate):
        pl.semaphore_signal(barrier, inc=1, device_id={"head": peer})

    loads[0].wait()
    pick = picks[...]
    eye = ones(iota((32, 32), 0) == iota((32, 32), 1))
    hi_t = nt(eye, lax.shift_right_logical(pick, 6).astype(F32).astype(BF))
    lo_t = nt(eye, (pick & 63).astype(F32).astype(BF))
    own_i = iota((CTX, ROWS), 0).astype(F32)
    blk_i = (iota((128, ROWS), 0) & 63).astype(F32)
    hi_oh = jnp.concatenate([ones(hi_t[j : j + 1] == own_i) for j in range(32)], axis=1)
    lo_oh = jnp.concatenate([ones(lo_t[j : j + 1] == blk_i) for j in range(32)], axis=1)
    flags = ones(nt(hi_oh, lo_oh) > 0.5)
    lane_r, lane_c = iota((128, 128), 0), iota((128, 128), 1)
    upto = ones((lane_r <= lane_c) & ((lane_r >> 6) == (lane_c >> 6)))
    rank = nn(flags, upto)
    hit = [(flags.astype(F32) > 0.5) & (rank == float(c + 1)) for c in range(CAP)]
    rep = ones((iota((CTX * 16, CTX), 0) >> 4) == iota((CTX * 16, CTX), 1))
    x0, x1, x2 = [nn(rep, ones(h)) for h in hit]
    row = iota((CTX * 16, 128), 0) & 15
    lane = iota((CTX * 16, 128), 1)
    last = jnp.where(lane < 64, x0, x1)
    first = jnp.where(row < 5, x0, jnp.where(row < 10, x1, jnp.where(row < 15, x2, last)))
    req_send[:, :128] = first.astype(BF)
    req_send[:, 128:] = jnp.where(row == 15, x2, 0.0).astype(BF)
    mine = pl.ds(pl.multiple_of(me * 16, 16), 16)
    req_recv[mine, :] = req_send[mine, :]

    pl.semaphore_wait(barrier, CTX - 1 + 3)

    def ask(k, carry):
        to = lax.rem(me + k, CTX)
        pltpu.make_async_remote_copy(
            src_ref=req_send.at[pl.ds(pl.multiple_of(to * 16, 16), 16), :],
            dst_ref=req_recv.at[mine, :],
            send_sem=req_sem.at[0],
            recv_sem=req_sem.at[1],
            device_id={"ctx": to},
        ).start()
        return carry

    lax.fori_loop(1, CTX, ask, 0)

    n_lane = nt(jnp.ones((8, 128), BF), flags) * 0.5
    wide_o, wide_l = iota((CTX, CTX * 16), 0), iota((CTX, CTX * 16), 1) >> 4
    count = nn(n_lane.astype(BF), ones(wide_o == wide_l))[:1]
    base = nn(n_lane.astype(BF), ones(wide_o < wide_l))[:1]
    row_l = iota((1, CTX * 16), 1) & 15
    slot_s = iota((SLOTS, CTX * 16), 0).astype(F32)

    def place(c, rows):
        return ones(jnp.where(rows & (c < count), base + c, -1.0) == slot_s)

    c_row = slot_of_row(row_l)
    part = row_l - 5 * c_row
    spread = jnp.concatenate(
        [place(c_row.astype(F32), (row_l < 15) & (part == i)) for i in range(5)], axis=0
    )
    rest = [place(float(c), row_l == 15) for c in range(CAP)]

    n_col = nn(flags, jnp.ones((128, 128), BF)) * 0.5
    before = ones(iota((CTX, CTX), 1) < iota((CTX, CTX), 0))
    base_col = nn(before, n_col.astype(BF))
    lane32 = iota((CTX, 128), 1)
    block_ids = jnp.zeros((1, 128), F32)
    for c in range(CAP):
        lo_c = jnp.sum(
            jnp.where(hit[c] & (lane32 < 64), lane32, 0).astype(F32), axis=1, keepdims=True
        )
        at = (base_col + float(c) == lane32.astype(F32)) & (n_col > float(c))
        ident = iota((CTX, 128), 0).astype(F32) * 64.0 + lo_c
        block_ids = block_ids + jnp.sum(jnp.where(at, ident, 0.0), axis=0, keepdims=True)
    ids = jnp.broadcast_to(block_ids, (ROWS, 128))
    pick_f = pick.astype(F32)
    found = jnp.zeros((ROWS, 128), F32)
    for j in range(32):
        found = jnp.where(pick_f[:, j : j + 1] == ids, 1.0, found)
    slot_l = iota((ROWS, 128), 1)
    hide = jnp.where((slot_l < SLOTS) & ((found < 0.5) | (slot_l >= POOL)), HIDE, 0.0).astype(BF)

    loads[1].wait()
    pltpu.make_async_remote_copy(
        src_ref=req_send.at[pl.ds(0, (CTX - 1) * 16), :],
        dst_ref=req_recv.at[pl.ds(0, (CTX - 1) * 16), :],
        send_sem=req_sem.at[0],
        recv_sem=req_sem.at[1],
        device_id={"ctx": me},
    ).wait_recv()
    got0, got1 = req_recv[:, :128], req_recv[:, 128:]
    part_r = row - 5 * slot_of_row(row)
    sel = [
        jnp.where((part_r == 2 * k + (lane >> 6)) & (row < 15), got0.astype(F32), 0.0).astype(BF)
        for k in range(3)
    ]
    tail_row = row == 15
    tail = [
        jnp.where(tail_row & (lane < 64), got0.astype(F32), 0.0).astype(BF),
        jnp.where(tail_row & (lane >= 64), got0.astype(F32), 0.0).astype(BF),
        jnp.where(tail_row & (lane < 64), got1.astype(F32), 0.0).astype(BF),
    ]
    base_sel = jnp.concatenate(sel, axis=1)

    def tile(u):
        return shard[:, u * 128 : u * 128 + 128]

    for g, (t0, n) in enumerate(GROUPS):
        for t in range(t0, t0 + n):
            src = [tile(5 * t + i) for i in range(5)] + [tile(35)]
            if t < 4:
                packed = nn(base_sel, jnp.concatenate(src, axis=0))
            else:
                packed = nn(
                    jnp.concatenate([base_sel, tail[t - 4]], axis=1),
                    jnp.concatenate(src + [tile(35)] * 2, axis=0),
                )
            pack_send[t] = packed.astype(BF)
        pack_recv[t0 : t0 + n, mine, :] = pack_send[t0 : t0 + n, mine, :]

        def give(k, carry, g=g, t0=t0, n=n):
            to = lax.rem(me + k, CTX)
            pltpu.make_async_remote_copy(
                src_ref=pack_send.at[pl.ds(t0, n), pl.ds(pl.multiple_of(to * 16, 16), 16), :],
                dst_ref=pack_recv.at[pl.ds(t0, n), mine, :],
                send_sem=pack_ssem.at[g],
                recv_sem=pack_rsem.at[g],
                device_id={"ctx": to},
            ).start()
            return carry

        lax.fori_loop(1, CTX, give, 0)

    loads[2].wait()
    loads[3].wait()
    lane_q = iota((ROWS, 128), 1)
    for pair in range(HEADS // 2):
        a, b, c = [
            qraw[:, (3 * pair + i) * 128 : (3 * pair + i + 1) * 128].astype(F32) for i in range(3)
        ]
        b_r, c_r = pltpu.roll(b, 64, 1), pltpu.roll(c, 64, 1)
        halves = (
            (a, jnp.where(lane_q < 64, b, b_r)),
            (jnp.where(lane_q < 64, b_r, c_r), jnp.where(lane_q < 64, c_r, c)),
        )
        for k, (nope, rope) in enumerate(halves):
            h = 2 * pair + k
            qext[h, :, :512] = nn(nope.astype(BF), kup[h]).astype(BF)
            qext[h, :, 512:640] = rope.astype(BF)
            qext[h, :, 640:] = hide
    slot_k = iota((8, SLOTS, 128), 1)
    lane_k = iota((8, SLOTS, 128), 2)
    for j in range(2):
        rext[j, :, 128:] = jnp.concatenate([ones(slot_k == lane_k).reshape(384, 128)] * 2, axis=0)

    def gather_copy(j, kind, piece, to):
        return pltpu.make_async_remote_copy(
            src_ref=pool.at[j, piece],
            dst_ref=pool.at[j, piece],
            send_sem=gat_ssem.at[j, kind],
            recv_sem=gat_rsem.at[j, kind],
            device_id={"head": to},
        )

    started = []

    def send(j, kind, piece, to):
        copy = gather_copy(j, kind, piece, to)
        copy.start()
        started.append(copy)

    tiles = {}
    lane48 = iota((SLOTS, 128), 1)

    def arrive(j):
        t0, n = GROUPS[j]
        pltpu.make_async_remote_copy(
            src_ref=pack_send.at[pl.ds(t0, n), pl.ds(0, (CTX - 1) * 16), :],
            dst_ref=pack_recv.at[pl.ds(t0, n), pl.ds(0, (CTX - 1) * 16), :],
            send_sem=pack_ssem.at[j],
            recv_sem=pack_rsem.at[j],
            device_id={"ctx": me},
        ).wait_recv()
        for t in range(t0, t0 + n):
            moved = nn(spread, pack_recv[t])
            for i in range(5):
                tiles[5 * t + i] = moved[SLOTS * i : SLOTS * i + SLOTS]
        if j == CHUNKS - 1:
            tiles[35] = sum(nn(rest[c], pack_recv[4 + c]) for c in range(CAP))
        w = [tiles[9 * j + i] for i in range(9)]
        r = [pltpu.roll(x, 64, 1) for x in w[4:]]
        cols = w[:4] + [jnp.where(lane48 < 64, r[k], r[k + 1]) for k in range(4)]
        cols.append(jnp.where(lane48 < 64, w[4], w[8]))
        pool[j, hd] = jnp.concatenate(cols, axis=1).astype(BF)
        send(j, 0, hd, up)
        send(j, 1, hd, down)
        send(j, 3, hd, mate)

    def relay_near(j):
        gather_copy(j, 0, down, up).wait_recv()
        gather_copy(j, 1, up, down).wait_recv()
        send(j, 2, lax.rem(hd + 6 + 4 * core, 8), lax.rem(hd + 2 + 4 * core, 8))
        send(j, 4, down, mate)
        send(j, 5, up, mate)

    def relay_far(j):
        gather_copy(j, 2, far, up).wait_recv()
        send(j, 6, far, mate)

    def ready(j):
        for kind in (3, 4, 5, 6):
            gather_copy(j, kind, mate, mate).wait_recv()
        rope = pool[j, :, :, 1024:].reshape(384, 128).astype(F32)
        lane_p = iota((384, 128), 1)
        rext[j % 2, :384, :128] = jnp.where(lane_p < 64, rope, 0.0).astype(BF)
        rext[j % 2, 384:, :128] = jnp.where(lane_p < 64, 0.0, rope).astype(BF)

    rows_step = HP * ROWS

    def attend(j, lo, hi):
        def step(n, carry):
            hs = pl.ds(n * HP, HP)
            keys = jnp.concatenate(
                [pool[j, :, :, :512].reshape(384, 512), pool[j, :, :, 512:1024].reshape(384, 512)],
                axis=0,
            )
            q = qext[hs].reshape(rows_step, 768)
            s = nt(q, jnp.concatenate([keys, rext[j % 2]], axis=1))
            m_new = jnp.broadcast_to(jnp.max(s, axis=1, keepdims=True), (rows_step, 128))
            if j > 0:
                m_old = top[hs].reshape(rows_step, 128)
                m_new = jnp.maximum(m_new, m_old)
            e = jnp.exp2((s - jnp.concatenate([m_new] * 6, axis=1)) * SCALE)
            part_sum = sum(e[:, 128 * k : 128 * k + 128] for k in range(6))
            o = nn(e.astype(BF), keys)
            if j > 0:
                alpha = jnp.exp2((m_old - m_new) * SCALE)
                part_sum = part_sum + total[hs].reshape(rows_step, 128) * alpha
                o = o + acc[hs].reshape(rows_step, 512) * jnp.concatenate([alpha] * 4, axis=1)
            if j < CHUNKS - 1:
                top[hs] = m_new.reshape(HP, ROWS, 128)
                total[hs] = part_sum.reshape(HP, ROWS, 128)
                acc[hs] = o.reshape(HP, ROWS, 512)
            else:
                mixed = (o / jnp.sum(part_sum, axis=1, keepdims=True)).astype(BF)
                for k in range(HP):
                    h = n * HP + k
                    out_ref[:, pl.ds(pl.multiple_of(h * 128, 128), 128)] = nn(
                        mixed[k * ROWS : (k + 1) * ROWS], vup[h]
                    ).astype(BF)
            return carry

        lax.fori_loop(lo, hi, step, 0)

    steps = HEADS // HP
    arrive(0)
    relay_near(0)
    relay_far(0)
    for j in range(CHUNKS):
        ready(j)
        if j == CHUNKS - 1:
            loads[4].wait()
            attend(j, 0, steps)
        else:
            attend(j, 0, steps // 4)
            arrive(j + 1)
            attend(j, steps // 4, steps // 2)
            relay_near(j + 1)
            attend(j, steps // 2, steps)
            relay_far(j + 1)

    for copy in started:
        copy.wait_send()
    pltpu.make_async_remote_copy(
        src_ref=req_send.at[pl.ds(0, (CTX - 1) * 16), :],
        dst_ref=req_recv.at[pl.ds(0, (CTX - 1) * 16), :],
        send_sem=req_sem.at[0],
        recv_sem=req_sem.at[1],
        device_id={"ctx": me},
    ).wait_send()
    for j, (t0, n) in enumerate(GROUPS):
        pltpu.make_async_remote_copy(
            src_ref=pack_send.at[pl.ds(t0, n), pl.ds(0, (CTX - 1) * 16), :],
            dst_ref=pack_recv.at[pl.ds(t0, n), pl.ds(0, (CTX - 1) * 16), :],
            send_sem=pack_ssem.at[j],
            recv_sem=pack_rsem.at[j],
            device_id={"ctx": me},
        ).wait_send()


def on_device(latent_cache, queries, chosen, key_up, value_up):
    any_spec = pl.BlockSpec(memory_space=pl.ANY)
    return pl.pallas_call(
        kernel,
        out_shape=jax.ShapeDtypeStruct((ROWS, HEADS * 128), BF),
        in_specs=[any_spec] * 5,
        out_specs=pl.BlockSpec(memory_space=pltpu.VMEM),
        scratch_shapes=[
            pltpu.VMEM((BD, SHARE), BF),
            pltpu.VMEM((ROWS, HEADS * 192), BF),
            pltpu.VMEM((ROWS, 32), jnp.int32),
            pltpu.VMEM((HEADS, 128, 512), BF),
            pltpu.VMEM((HEADS, 512, 128), BF),
            pltpu.VMEM((CTX * 16, 256), BF),
            pltpu.VMEM((CTX * 16, 256), BF),
            pltpu.VMEM((7, CTX * 16, 128), BF),
            pltpu.VMEM((7, CTX * 16, 128), BF),
            pltpu.VMEM((CHUNKS, 8, SLOTS, PAIR), BF),
            pltpu.VMEM((2, KEYS, 256), BF),
            pltpu.VMEM((HEADS, ROWS, 768), BF),
            pltpu.VMEM((HEADS, ROWS, 512), F32),
            pltpu.VMEM((HEADS, ROWS, 128), F32),
            pltpu.VMEM((HEADS, ROWS, 128), F32),
            pltpu.SemaphoreType.DMA((5,)),
            pltpu.SemaphoreType.DMA((2,)),
            pltpu.SemaphoreType.DMA((CHUNKS,)),
            pltpu.SemaphoreType.DMA((CHUNKS,)),
            pltpu.SemaphoreType.DMA((CHUNKS, 7)),
            pltpu.SemaphoreType.DMA((CHUNKS, 7)),
        ],
        compiler_params=pltpu.CompilerParams(
            collective_id=0, has_side_effects=True, vmem_limit_bytes=56 * 1024 * 1024
        ),
        cost_estimate=pl.CostEstimate(
            flops=15_000_000_000, bytes_accessed=8_000_000, transcendentals=6_300_000
        ),
        name="sparse_latent_attention",
    )(latent_cache, queries, chosen, key_up, value_up)


def solution(mesh):
    return jax.shard_map(
        on_device,
        mesh=mesh,
        in_specs=(
            P("ctx", None),
            P("ctx", "head"),
            P("ctx", None),
            P("head", None, None),
            P("head", None, None),
        ),
        out_specs=P("ctx", "head"),
        check_vma=False,
    )
```

```python
import functools

import jax
import jax.numpy as jnp
from jax import lax
from jax.experimental import pallas as pl
from jax.experimental.pallas import tpu as pltpu
from jax.sharding import PartitionSpec as P

BF = jnp.bfloat16
F32 = jnp.float32
CTX = 32
HEADS = 16
ROWS = 128
BD = 64
CAP = 3
POOL = 44
SLOTS = 48
SHARE = 4608
PAIR = 1152
CHUNKS = 4
KEYS = 768
GROUPS = ((0, 1), (1, 1), (2, 2), (4, 2), (6, 1))
AHEAD = 3
HP = 8
HIDE = -1e30
SCALE = (192**-0.5) * 1.4426950408889634


def nn(a, b):
    return lax.dot_general(a, b, (((1,), (0,)), ((), ())), preferred_element_type=F32)


def nt(a, b):
    return lax.dot_general(a, b, (((1,), (1,)), ((), ())), preferred_element_type=F32)


def iota(shape, dim):
    return lax.broadcasted_iota(jnp.int32, shape, dim)


def ones(cond):
    return jnp.where(cond, 1.0, 0.0).astype(BF)


def slot_of_row(r):
    return jnp.where(r < 5, 0, jnp.where(r < 10, 1, 2))


def kernel(
    cache_hbm, queries_hbm, chosen_hbm, kup_hbm, vup_hbm, out_ref,
    shard, qraw, picks, kup, vup, req_send, req_recv, pack_send, pack_recv,
    pool, first, rext, qext, acc, top, total,
    in_sem, req_sem, pack_ssem, pack_rsem, gat_ssem, gat_rsem,
):
    me = lax.axis_index("ctx")
    hd = lax.axis_index("head")
    core = lax.rem(hd, 2)
    up = lax.rem(hd + 2, 8)
    down = lax.rem(hd + 6, 8)
    mate = hd + 1 - 2 * core
    far = lax.rem(hd + 4, 8)

    loads = []
    for n, (src, dst) in enumerate(
        (
            (chosen_hbm, picks),
            (cache_hbm.at[:, pl.ds(pl.multiple_of(hd * SHARE, 128), SHARE)], shard),
            (queries_hbm, qraw),
            (kup_hbm, kup),
            (vup_hbm, vup),
        )
    ):
        load = pltpu.make_async_copy(src, dst, in_sem.at[n])
        load.start()
        loads.append(load)

    barrier = pltpu.get_barrier_semaphore()

    def greet(k, carry):
        pl.semaphore_signal(barrier, inc=1, device_id={"ctx": lax.rem(me + k, CTX)})
        return carry

    lax.fori_loop(1, CTX, greet, 0)
    for peer in (up, down, far, mate):
        pl.semaphore_signal(barrier, inc=1, device_id={"head": peer})

    loads[0].wait()
    pick = picks[...]
    hi, lo = lax.shift_right_logical(pick, 6), pick & 63
    own_i = iota((CTX, ROWS), 0)
    blk_i = iota((128, ROWS), 0) & 63
    hi_oh = jnp.concatenate([ones(hi[j : j + 1] == own_i) for j in range(32)], axis=1)
    lo_oh = jnp.concatenate([ones(lo[j : j + 1] == blk_i) for j in range(32)], axis=1)
    flags = ones(nt(hi_oh, lo_oh) > 0.5)
    lane_r, lane_c = iota((128, 128), 0), iota((128, 128), 1)
    upto = ones((lane_r <= lane_c) & ((lane_r >> 6) == (lane_c >> 6)))
    rank = nn(flags, upto)
    hit = [(flags.astype(F32) > 0.5) & (rank == float(c + 1)) for c in range(CAP)]
    rep = ones((iota((CTX * 16, CTX), 0) >> 4) == iota((CTX * 16, CTX), 1))
    x0, x1, x2 = [nn(rep, ones(h)) for h in hit]
    row = iota((CTX * 16, 128), 0) & 15
    lane = iota((CTX * 16, 128), 1)
    req_send[...] = jnp.where(row < 5, x0, jnp.where(row < 10, x1, x2)).astype(BF)
    mine = pl.ds(pl.multiple_of(me * 16, 16), 16)
    req_recv[mine, :] = req_send[mine, :]

    pl.semaphore_wait(barrier, CTX - 1 + 4)

    def ask(k, carry):
        to = lax.rem(me + k, CTX)
        pltpu.make_async_remote_copy(
            src_ref=req_send.at[pl.ds(pl.multiple_of(to * 16, 16), 16), :],
            dst_ref=req_recv.at[mine, :],
            send_sem=req_sem.at[0],
            recv_sem=req_sem.at[1],
            device_id={"ctx": to},
        ).start()
        return carry

    lax.fori_loop(1, CTX, ask, 0)

    n_lane = nt(jnp.ones((8, 128), BF), flags) * 0.5
    wide_o, wide_l = iota((CTX, CTX * 16), 0), iota((CTX, CTX * 16), 1) >> 4
    count = nn(n_lane.astype(BF), ones(wide_o == wide_l))[:1]
    base = nn(n_lane.astype(BF), ones(wide_o < wide_l))[:1]
    row_l = iota((1, CTX * 16), 1) & 15
    slot_s = iota((SLOTS, CTX * 16), 0).astype(F32)

    def place(c, rows):
        return ones(jnp.where(rows & (c < count), base + c, -1.0) == slot_s)

    c_row = slot_of_row(row_l)
    part = row_l - 5 * c_row
    spread = jnp.concatenate(
        [place(c_row.astype(F32), (row_l < 15) & (part == i)) for i in range(5)], axis=0
    )
    rest = [place(float(c), row_l == 15) for c in range(CAP)]

    n_row = n_lane[:1]
    base_row = nn(n_lane.astype(BF), ones(iota((CTX, CTX), 0) < iota((CTX, CTX), 1)))[:1]
    lane_v = iota((8, 128), 1)
    block_v = jnp.where(lane_v < 64, lane_v, 0).astype(F32).astype(BF)
    slot_c = iota((SLOTS, CTX), 0).astype(F32)
    owner_v = iota((1, CTX), 1).astype(F32) * 64.0
    ids = jnp.zeros((SLOTS, CTX), F32)
    for c in range(CAP):
        ident = owner_v + nt(block_v, ones(hit[c]))[:1]
        at = jnp.where(float(c) < n_row, base_row + float(c), -1.0) == slot_c
        ids = ids + jnp.where(at, ident, 0.0)
    ids = jnp.broadcast_to(jnp.sum(ids, axis=1, keepdims=True), (SLOTS, ROWS))
    pick_f = pick.astype(F32)
    found = jnp.zeros((SLOTS, ROWS), F32)
    for j in range(32):
        found = jnp.where(pick_f[j : j + 1] == ids, 1.0, found)
    hidden = jnp.where((found < 0.5) | (iota((SLOTS, ROWS), 0) >= POOL), HIDE, 0.0)
    hide = jnp.concatenate([hidden, jnp.zeros((ROWS - SLOTS, ROWS), F32)], axis=0).T.astype(BF)

    loads[2].wait()
    loads[3].wait()
    lane_q = iota((ROWS, 128), 1)
    for pair in range(HEADS // 2):
        a, b, c = [
            qraw[:, (3 * pair + i) * 128 : (3 * pair + i + 1) * 128].astype(F32) for i in range(3)
        ]
        b_r, c_r = pltpu.roll(b, 64, 1), pltpu.roll(c, 64, 1)
        halves = (
            (a, jnp.where(lane_q < 64, b, b_r)),
            (jnp.where(lane_q < 64, b_r, c_r), jnp.where(lane_q < 64, c_r, c)),
        )
        for k, (nope, rope) in enumerate(halves):
            h = 2 * pair + k
            qext[h, :, :512] = nn(nope.astype(BF), kup[h]).astype(BF)
            qext[h, :, 512:640] = rope.astype(BF)
            qext[h, :, 640:] = hide
    slot_k = iota((8, SLOTS, 128), 1)
    lane_k = iota((8, SLOTS, 128), 2)
    for j in range(2):
        rext[j, :, 128:] = jnp.concatenate([ones(slot_k == lane_k).reshape(384, 128)] * 2, axis=0)

    loads[1].wait()
    pltpu.make_async_remote_copy(
        src_ref=req_send.at[pl.ds(0, (CTX - 1) * 16), :],
        dst_ref=req_recv.at[pl.ds(0, (CTX - 1) * 16), :],
        send_sem=req_sem.at[0],
        recv_sem=req_sem.at[1],
        device_id={"ctx": me},
    ).wait_recv()
    got = req_recv[...].astype(F32)
    part_r = row - 5 * slot_of_row(row)
    sel = [
        jnp.where((part_r == 2 * k + (lane >> 6)) & (row < 15), got, 0.0).astype(BF)
        for k in range(3)
    ]
    tail = [
        jnp.where((row == 15) & (lane < 64), pltpu.roll(got, 15 - 5 * c, 0), 0.0).astype(BF)
        for c in range(CAP)
    ]
    base_sel = jnp.concatenate(sel, axis=1)

    def tile(u):
        return shard[:, u * 128 : u * 128 + 128]

    def give(g):
        t0, n = GROUPS[g]

        def one(k, carry):
            to = lax.rem(me + k, CTX)
            pltpu.make_async_remote_copy(
                src_ref=pack_send.at[pl.ds(t0, n), pl.ds(pl.multiple_of(to * 16, 16), 16), :],
                dst_ref=pack_recv.at[pl.ds(t0, n), mine, :],
                send_sem=pack_ssem.at[g],
                recv_sem=pack_rsem.at[g],
                device_id={"ctx": to},
            ).start()
            return carry

        lax.fori_loop(1, CTX, one, 0)

    for g, (t0, n) in enumerate(GROUPS):
        for t in range(t0, t0 + n):
            src = [tile(5 * t + i) for i in range(5)] + [tile(35)]
            if t < 4:
                packed = nn(base_sel, jnp.concatenate(src, axis=0))
            else:
                packed = nn(
                    jnp.concatenate([base_sel, tail[t - 4]], axis=1),
                    jnp.concatenate(src + [tile(35)] * 2, axis=0),
                )
            pack_send[t] = packed.astype(BF)
        pack_recv[t0 : t0 + n, mine, :] = pack_send[t0 : t0 + n, mine, :]
        if g < AHEAD:
            give(g)


    def gather_copy(g, kind, piece, to):
        part = first.at[g, piece] if g < 2 else pool.at[g - 2, piece]
        return pltpu.make_async_remote_copy(
            src_ref=part,
            dst_ref=part,
            send_sem=gat_ssem.at[g, kind],
            recv_sem=gat_rsem.at[g, kind],
            device_id={"head": to},
        )

    started = []

    def send(g, kind, piece, to):
        copy = gather_copy(g, kind, piece, to)
        copy.start()
        started.append(copy)

    tiles = {}
    lane48 = iota((SLOTS, 128), 1)

    def arrive(g):
        t0, n = GROUPS[g]
        pltpu.make_async_remote_copy(
            src_ref=pack_send.at[pl.ds(t0, n), pl.ds(0, (CTX - 1) * 16), :],
            dst_ref=pack_recv.at[pl.ds(t0, n), pl.ds(0, (CTX - 1) * 16), :],
            send_sem=pack_ssem.at[g],
            recv_sem=pack_rsem.at[g],
            device_id={"ctx": me},
        ).wait_recv()
        for t in range(t0, t0 + n):
            moved = nn(spread, pack_recv[t])
            for i in range(5):
                tiles[5 * t + i] = moved[SLOTS * i : SLOTS * i + SLOTS]
        if g == len(GROUPS) - 1:
            tiles[35] = sum(nn(rest[c], pack_recv[4 + c]) for c in range(CAP))
        u = 9 * max(g - 1, 0)
        even = [tiles[u + k] for k in range(4)]
        if g > 0:
            r = [pltpu.roll(tiles[u + k], 64, 1) for k in range(4, 9)]
            odd = [jnp.where(lane48 < 64, r[k], r[k + 1]) for k in range(4)]
        if g == 0:
            cols = even + [jnp.where(lane48 < 64, tiles[4], 0.0)]
            first[0, hd] = jnp.concatenate(cols, axis=1).astype(BF)
        elif g == 1:
            cols = odd + [jnp.where(lane48 < 64, 0.0, tiles[8])]
            first[1, hd] = jnp.concatenate(cols, axis=1).astype(BF)
        else:
            cols = even + odd + [jnp.where(lane48 < 64, tiles[u + 4], tiles[u + 8])]
            pool[g - 2, hd] = jnp.concatenate(cols, axis=1).astype(BF)
        send(g, 0, hd, up)
        send(g, 1, hd, down)
        send(g, 2, hd, far)
        send(g, 3, hd, mate)
        if g + AHEAD < len(GROUPS):
            give(g + AHEAD)

    def relay(g):
        for kind, piece in ((0, down), (1, up), (2, far)):
            gather_copy(g, kind, piece, piece).wait_recv()
            send(g, 4 + kind, piece, mate)

    def ready(j):
        for g in (0, 1) if j == 0 else (j + 1,):
            for kind in (3, 4, 5, 6):
                gather_copy(g, kind, mate, mate).wait_recv()
        if j == 0:
            rext[0, :384, :128] = first[0, :, :, 512:].reshape(384, 128)
            rext[0, 384:, :128] = first[1, :, :, 512:].reshape(384, 128)
        else:
            rope = pool[j - 1, :, :, 1024:].reshape(384, 128).astype(F32)
            lane_p = iota((384, 128), 1)
            rext[j % 2, :384, :128] = jnp.where(lane_p < 64, rope, 0.0).astype(BF)
            rext[j % 2, 384:, :128] = jnp.where(lane_p < 64, 0.0, rope).astype(BF)

    rows_step = HP * ROWS

    def attend(j, n):
        hs = pl.ds(n * HP, HP)
        if j == 0:
            halves = [first[0, :, :, :512], first[1, :, :, :512]]
        else:
            halves = [pool[j - 1, :, :, :512], pool[j - 1, :, :, 512:1024]]
        keys = jnp.concatenate([x.reshape(384, 512) for x in halves], axis=0)
        q = qext[hs].reshape(rows_step, 768)
        s = nt(q, jnp.concatenate([keys, rext[j % 2]], axis=1))
        m_new = jnp.broadcast_to(jnp.max(s, axis=1, keepdims=True), (rows_step, 128))
        if j > 0:
            m_old = top[hs].reshape(rows_step, 128)
            m_new = jnp.maximum(m_new, m_old)
        e = jnp.exp2((s - jnp.concatenate([m_new] * 6, axis=1)) * SCALE)
        part_sum = sum(e[:, 128 * k : 128 * k + 128] for k in range(6))
        o = nn(e.astype(BF), keys)
        if j > 0:
            alpha = jnp.exp2((m_old - m_new) * SCALE)
            part_sum = part_sum + total[hs].reshape(rows_step, 128) * alpha
            o = o + acc[hs].reshape(rows_step, 512) * jnp.concatenate([alpha] * 4, axis=1)
        if j < CHUNKS - 1:
            top[hs] = m_new.reshape(HP, ROWS, 128)
            total[hs] = part_sum.reshape(HP, ROWS, 128)
            acc[hs] = o.reshape(HP, ROWS, 512)
        else:
            mixed = (o / jnp.sum(part_sum, axis=1, keepdims=True)).astype(BF)
            for k in range(HP):
                h = n * HP + k
                out_ref[:, pl.ds(pl.multiple_of(h * 128, 128), 128)] = nn(
                    mixed[k * ROWS : (k + 1) * ROWS], vup[h]
                ).astype(BF)

    arrive(0)
    arrive(1)
    relay(0)
    arrive(2)
    relay(1)
    ready(0)
    attend(0, 0)
    arrive(3)
    attend(0, 1)
    relay(2)
    arrive(4)
    ready(1)
    attend(1, 0)
    relay(3)
    attend(1, 1)
    ready(2)
    attend(2, 0)
    relay(4)
    attend(2, 1)
    ready(3)
    loads[4].wait()
    attend(3, 0)
    attend(3, 1)

    for copy in started:
        copy.wait_send()
    pltpu.make_async_remote_copy(
        src_ref=req_send.at[pl.ds(0, (CTX - 1) * 16), :],
        dst_ref=req_recv.at[pl.ds(0, (CTX - 1) * 16), :],
        send_sem=req_sem.at[0],
        recv_sem=req_sem.at[1],
        device_id={"ctx": me},
    ).wait_send()
    for j, (t0, n) in enumerate(GROUPS):
        pltpu.make_async_remote_copy(
            src_ref=pack_send.at[pl.ds(t0, n), pl.ds(0, (CTX - 1) * 16), :],
            dst_ref=pack_recv.at[pl.ds(t0, n), pl.ds(0, (CTX - 1) * 16), :],
            send_sem=pack_ssem.at[j],
            recv_sem=pack_rsem.at[j],
            device_id={"ctx": me},
        ).wait_send()


def on_device(latent_cache, queries, chosen, key_up, value_up):
    any_spec = pl.BlockSpec(memory_space=pl.ANY)
    return pl.pallas_call(
        kernel,
        out_shape=jax.ShapeDtypeStruct((ROWS, HEADS * 128), BF),
        in_specs=[any_spec] * 5,
        out_specs=pl.BlockSpec(memory_space=pltpu.VMEM),
        scratch_shapes=[
            pltpu.VMEM((BD, SHARE), BF),
            pltpu.VMEM((ROWS, HEADS * 192), BF),
            pltpu.VMEM((32, ROWS), jnp.int32),
            pltpu.VMEM((HEADS, 128, 512), BF),
            pltpu.VMEM((HEADS, 512, 128), BF),
            pltpu.VMEM((CTX * 16, 128), BF),
            pltpu.VMEM((CTX * 16, 128), BF),
            pltpu.VMEM((7, CTX * 16, 128), BF),
            pltpu.VMEM((7, CTX * 16, 128), BF),
            pltpu.VMEM((CHUNKS - 1, 8, SLOTS, PAIR), BF),
            pltpu.VMEM((2, 8, SLOTS, 640), BF),
            pltpu.VMEM((2, KEYS, 256), BF),
            pltpu.VMEM((HEADS, ROWS, 768), BF),
            pltpu.VMEM((HEADS, ROWS, 512), F32),
            pltpu.VMEM((HEADS, ROWS, 128), F32),
            pltpu.VMEM((HEADS, ROWS, 128), F32),
            pltpu.SemaphoreType.DMA((5,)),
            pltpu.SemaphoreType.DMA((2,)),
            pltpu.SemaphoreType.DMA((len(GROUPS),)),
            pltpu.SemaphoreType.DMA((len(GROUPS),)),
            pltpu.SemaphoreType.DMA((len(GROUPS), 7)),
            pltpu.SemaphoreType.DMA((len(GROUPS), 7)),
        ],
        compiler_params=pltpu.CompilerParams(
            collective_id=0, has_side_effects=True, vmem_limit_bytes=56 * 1024 * 1024
        ),
        cost_estimate=pl.CostEstimate(
            flops=15_000_000_000, bytes_accessed=8_000_000, transcendentals=6_300_000
        ),
        name="sparse_latent_attention",
    )(latent_cache, queries, chosen.T, key_up, value_up)


def solution(mesh):
    return jax.shard_map(
        on_device,
        mesh=mesh,
        in_specs=(
            P("ctx", None),
            P("ctx", "head"),
            P("ctx", None),
            P("head", None, None),
            P("head", None, None),
        ),
        out_specs=P("ctx", "head"),
        check_vma=False,
    )
```

```python
import functools

import jax
import jax.numpy as jnp
from jax import lax
from jax.experimental import pallas as pl
from jax.experimental.pallas import tpu as pltpu
from jax.sharding import PartitionSpec as P

BF = jnp.bfloat16
F32 = jnp.float32
CTX = 32
HEADS = 16
ROWS = 128
BD = 64
CAP = 3
POOL = 44
SLOTS = 48
SHARE = 4608
KEYS = 8 * SLOTS
CHUNKS = ((0, 1), (2, 3), (4,), (5, 6), (7,))
TILES = 7
AHEAD = 3
HP = 8
HIDE = -1e30
SCALE = (192**-0.5) * 1.4426950408889634


def nn(a, b):
    return lax.dot_general(a, b, (((1,), (0,)), ((), ())), preferred_element_type=F32)


def nt(a, b):
    return lax.dot_general(a, b, (((1,), (1,)), ((), ())), preferred_element_type=F32)


def iota(shape, dim):
    return lax.broadcasted_iota(jnp.int32, shape, dim)


def ones(cond):
    return jnp.where(cond, 1.0, 0.0).astype(BF)


def slot_of_row(r):
    return jnp.where(r < 5, 0, jnp.where(r < 10, 1, 2))


def kernel(
    cache_hbm, queries_hbm, chosen_hbm, kup_hbm, vup_hbm, out_hbm,
    shard, qraw, picks, kup, vup, req_send, req_recv, pack_send, pack_recv,
    pool, slot_oh, qext, acc, top, total, result,
    in_sem, req_sem, pack_ssem, pack_rsem, gat_ssem, gat_rsem, out_sem,
):
    me = lax.axis_index("ctx")
    hd = lax.axis_index("head")
    core = lax.rem(hd, 2)
    up = lax.rem(hd + 2, 8)
    down = lax.rem(hd + 6, 8)
    mate = hd + 1 - 2 * core
    far = lax.rem(hd + 4, 8)

    loads = []
    for n, (src, dst) in enumerate(
        (
            (chosen_hbm, picks),
            (cache_hbm.at[:, pl.ds(pl.multiple_of(hd * SHARE, 128), SHARE)], shard),
            (queries_hbm, qraw),
            (kup_hbm, kup),
            (vup_hbm, vup),
        )
    ):
        load = pltpu.make_async_copy(src, dst, in_sem.at[n])
        load.start()
        loads.append(load)

    barrier = pltpu.get_barrier_semaphore()

    def greet(k, carry):
        pl.semaphore_signal(barrier, inc=1, device_id={"ctx": lax.rem(me + k, CTX)})
        return carry

    lax.fori_loop(1, CTX, greet, 0)
    for peer in (up, down, far, mate):
        pl.semaphore_signal(barrier, inc=1, device_id={"head": peer})

    loads[0].wait()
    pick = picks[...]
    hi, lo = lax.shift_right_logical(pick, 6), pick & 63
    own_i = iota((CTX, ROWS), 0)
    blk_i = iota((128, ROWS), 0) & 63
    hi_oh = jnp.concatenate([ones(hi[j : j + 1] == own_i) for j in range(32)], axis=1)
    lo_oh = jnp.concatenate([ones(lo[j : j + 1] == blk_i) for j in range(32)], axis=1)
    flags = ones(nt(hi_oh, lo_oh) > 0.5)
    lane_r, lane_c = iota((128, 128), 0), iota((128, 128), 1)
    upto = ones((lane_r <= lane_c) & ((lane_r >> 6) == (lane_c >> 6)))
    rank = nn(flags, upto)
    hit = [(flags.astype(F32) > 0.5) & (rank == float(c + 1)) for c in range(CAP)]
    order = jnp.where(flags.astype(F32) > 0.5, rank, 0.0)
    for o in range(CTX):
        req_send[o] = order[o : o + 1]
    req_recv[me] = req_send[me]
    mine = pl.ds(pl.multiple_of(me * 16, 16), 16)

    pl.semaphore_wait(barrier, CTX - 1 + 4)

    def ask(k, carry):
        to = lax.rem(me + k, CTX)
        pltpu.make_async_remote_copy(
            src_ref=req_send.at[to],
            dst_ref=req_recv.at[me],
            send_sem=req_sem.at[0],
            recv_sem=req_sem.at[1],
            device_id={"ctx": to},
        ).start()
        return carry

    lax.fori_loop(1, CTX, ask, 0)

    n_lane = nt(jnp.ones((8, 128), BF), flags) * 0.5
    wide_o, wide_l = iota((CTX, CTX * 16), 0), iota((CTX, CTX * 16), 1) >> 4
    count = nn(n_lane.astype(BF), ones(wide_o == wide_l))[:1]
    base = nn(n_lane.astype(BF), ones(wide_o < wide_l))[:1]
    row_l = iota((1, CTX * 16), 1) & 15
    slot_s = iota((SLOTS, CTX * 16), 0).astype(F32)

    def place(c, rows):
        return ones(jnp.where(rows & (c < count), base + c, -1.0) == slot_s)

    c_row = slot_of_row(row_l)
    part = row_l - 5 * c_row
    spread = jnp.concatenate(
        [place(c_row.astype(F32), (row_l < 15) & (part == i)) for i in range(5)], axis=0
    )
    rest = [place(float(c), row_l == 15) for c in range(CAP)]

    n_row = n_lane[:1]
    base_row = nn(n_lane.astype(BF), ones(iota((CTX, CTX), 0) < iota((CTX, CTX), 1)))[:1]
    lane_v = iota((8, 128), 1)
    block_v = jnp.where(lane_v < 64, lane_v, 0).astype(F32).astype(BF)
    slot_c = iota((SLOTS, CTX), 0).astype(F32)
    owner_v = iota((1, CTX), 1).astype(F32) * 64.0
    ids = jnp.zeros((SLOTS, CTX), F32)
    for c in range(CAP):
        ident = owner_v + nt(block_v, ones(hit[c]))[:1]
        at = jnp.where(float(c) < n_row, base_row + float(c), -1.0) == slot_c
        ids = ids + jnp.where(at, ident, 0.0)
    ids = jnp.broadcast_to(jnp.sum(ids, axis=1, keepdims=True), (SLOTS, ROWS))
    pick_f = pick.astype(F32)
    found = jnp.zeros((SLOTS, ROWS), F32)
    for j in range(32):
        found = jnp.where(pick_f[j : j + 1] == ids, 1.0, found)
    hidden = jnp.where((found < 0.5) | (iota((SLOTS, ROWS), 0) >= POOL), HIDE, 0.0)
    hide = jnp.concatenate([hidden, jnp.zeros((ROWS - SLOTS, ROWS), F32)], axis=0).T.astype(BF)

    loads[2].wait()
    loads[3].wait()
    lane_q = iota((ROWS, 128), 1)
    for pair in range(HEADS // 2):
        a, b, c = [
            qraw[:, (3 * pair + i) * 128 : (3 * pair + i + 1) * 128].astype(F32) for i in range(3)
        ]
        b_r, c_r = pltpu.roll(b, 64, 1), pltpu.roll(c, 64, 1)
        halves = (
            (a, jnp.where(lane_q < 64, b, b_r)),
            (jnp.where(lane_q < 64, b_r, c_r), jnp.where(lane_q < 64, c_r, c)),
        )
        for k, (nope, rope) in enumerate(halves):
            h = 2 * pair + k
            qext[h, :, :512] = nn(nope.astype(BF), kup[h]).astype(BF)
            qext[h, :, 512:640] = rope.astype(BF)
            qext[h, :, 640:] = hide
    slot_oh[...] = ones(iota((8, SLOTS, 128), 1) == iota((8, SLOTS, 128), 2)).reshape(KEYS, 128)

    loads[1].wait()
    pltpu.make_async_remote_copy(
        src_ref=req_send.at[pl.ds(0, CTX - 1)],
        dst_ref=req_recv.at[pl.ds(0, CTX - 1)],
        send_sem=req_sem.at[0],
        recv_sem=req_sem.at[1],
        device_id={"ctx": me},
    ).wait_recv()
    rep = ones((iota((CTX * 16, CTX), 0) >> 4) == iota((CTX * 16, CTX), 1))
    got = nn(rep, req_recv[:, 0, :].astype(BF))
    row = iota((CTX * 16, 128), 0) & 15
    lane = iota((CTX * 16, 128), 1)
    c_of = slot_of_row(row)
    asked = (got == (c_of + 1).astype(F32)) & (row < 15)
    sel = [ones(asked & (row - 5 * c_of == 2 * k + (lane >> 6))) for k in range(3)]
    spare = [ones((row == 15) & (lane >= 64) & (got == float(c + 1))) for c in range(CAP)]

    def tile(u):
        return shard[:, u * 128 : u * 128 + 128]

    def give(t):
        def one(k, carry):
            to = lax.rem(me + k, CTX)
            pltpu.make_async_remote_copy(
                src_ref=pack_send.at[t, pl.ds(pl.multiple_of(to * 16, 16), 16), :],
                dst_ref=pack_recv.at[t, mine, :],
                send_sem=pack_ssem.at[t],
                recv_sem=pack_rsem.at[t],
                device_id={"ctx": to},
            ).start()
            return carry

        lax.fori_loop(1, CTX, one, 0)

    for t in range(TILES):
        if t < 6:
            last = sel[2] + spare[t % 3]
            src = [tile(5 * t + i) for i in range(5)] + [tile(30 + t // 3)]
        else:
            last = sel[2]
            src = [tile(min(32 + i, 35)) for i in range(6)]
        packed = nn(jnp.concatenate(sel[:2] + [last], axis=1), jnp.concatenate(src, axis=0))
        pack_send[t] = packed.astype(BF)
        pack_recv[t, mine, :] = pack_send[t, mine, :]
        if t < AHEAD:
            give(t)

    def gather_copy(p, kind, piece, to):
        part = pool.at[p, piece]
        return pltpu.make_async_remote_copy(
            src_ref=part,
            dst_ref=part,
            send_sem=gat_ssem.at[p, kind],
            recv_sem=gat_rsem.at[p, kind],
            device_id={"head": to},
        )

    started = []

    def send(p, kind, piece, to):
        copy = gather_copy(p, kind, piece, to)
        copy.start()
        started.append(copy)

    tiles = {}
    lane48 = iota((SLOTS, 128), 1)

    def share(p):
        u = 9 * (p // 2)
        if p % 2 == 0:
            cols = [tiles[u + k] for k in range(4)]
            cols.append(jnp.where(lane48 < 64, tiles[u + 4], 0.0))
        else:
            r = [pltpu.roll(tiles[u + k], 64, 1) for k in range(4, 9)]
            cols = [jnp.where(lane48 < 64, r[k], r[k + 1]) for k in range(4)]
            cols.append(jnp.where(lane48 < 64, 0.0, tiles[u + 8]))
        pool[p, hd] = jnp.concatenate(cols, axis=1).astype(BF)
        send(p, 0, hd, up)
        send(p, 1, hd, down)
        send(p, 2, hd, far)
        send(p, 3, hd, mate)

    def arrive(t):
        pltpu.make_async_remote_copy(
            src_ref=pack_send.at[t, pl.ds(0, (CTX - 1) * 16), :],
            dst_ref=pack_recv.at[t, pl.ds(0, (CTX - 1) * 16), :],
            send_sem=pack_ssem.at[t],
            recv_sem=pack_rsem.at[t],
            device_id={"ctx": me},
        ).wait_recv()
        if t + AHEAD < TILES:
            give(t + AHEAD)
        moved = nn(spread, pack_recv[t])
        for i in range(5):
            tiles[5 * t + i if t < 6 else 32 + i] = moved[SLOTS * i : SLOTS * i + SLOTS]
        if t == 5:
            for k in range(2):
                tiles[30 + k] = sum(nn(rest[c], pack_recv[3 * k + c]) for c in range(CAP))
        for p in ((0,), (1,), (2,), (3,), (4,), (5, 6), (7,))[t]:
            share(p)

    def relay(p):
        for kind, piece in ((0, down), (1, up), (2, far)):
            gather_copy(p, kind, piece, piece).wait_recv()
            send(p, 4 + kind, piece, mate)

    def ready(j):
        for p in CHUNKS[j]:
            for kind in (3, 4, 5, 6):
                gather_copy(p, kind, mate, mate).wait_recv()

    def store_head(h):
        lanes = pl.ds(h * 128, 128)
        return pltpu.make_async_copy(result.at[:, lanes], out_hbm.at[:, lanes], out_sem.at[h])

    rows_step = HP * ROWS

    def attend(j, n):
        hs = pl.ds(n * HP, HP)
        wide = len(CHUNKS[j]) * KEYS // 128
        held = [pool[p].reshape(KEYS, 640) for p in CHUNKS[j]]
        whole = jnp.concatenate(
            [jnp.concatenate([x, slot_oh[...]], axis=1) for x in held], axis=0
        )
        keys = jnp.concatenate([x[:, :512] for x in held], axis=0)
        q = qext[hs].reshape(rows_step, 768)
        s = nt(q, whole)
        m_new = jnp.broadcast_to(jnp.max(s, axis=1, keepdims=True), (rows_step, 128))
        if j > 0:
            m_old = top[hs].reshape(rows_step, 128)
            m_new = jnp.maximum(m_new, m_old)
        e = jnp.exp2((s - jnp.concatenate([m_new] * wide, axis=1)) * SCALE)
        part_sum = sum(e[:, 128 * k : 128 * k + 128] for k in range(wide))
        o = nn(e.astype(BF), keys)
        if j > 0:
            alpha = jnp.exp2((m_old - m_new) * SCALE)
            part_sum = part_sum + total[hs].reshape(rows_step, 128) * alpha
            o = o + acc[hs].reshape(rows_step, 512) * jnp.concatenate([alpha] * 4, axis=1)
        if j < len(CHUNKS) - 1:
            top[hs] = m_new.reshape(HP, ROWS, 128)
            total[hs] = part_sum.reshape(HP, ROWS, 128)
            acc[hs] = o.reshape(HP, ROWS, 512)
        else:
            mixed = (o * (1.0 / jnp.sum(part_sum, axis=1, keepdims=True))).astype(BF)
            for k in range(HP):
                h = n * HP + k
                result[:, h * 128 : h * 128 + 128] = nn(
                    mixed[k * ROWS : (k + 1) * ROWS], vup[h]
                ).astype(BF)
                store_head(h).start()

    arrive(0)
    arrive(1)
    relay(0)
    arrive(2)
    relay(1)
    arrive(3)
    ready(0)
    attend(0, 0)
    relay(2)
    arrive(4)
    attend(0, 1)
    relay(3)
    arrive(5)
    ready(1)
    attend(1, 0)
    relay(4)
    arrive(6)
    attend(1, 1)
    relay(5)
    relay(6)
    ready(2)
    attend(2, 0)
    attend(2, 1)
    relay(7)
    ready(3)
    attend(3, 0)
    attend(3, 1)
    ready(4)
    loads[4].wait()
    attend(4, 0)
    attend(4, 1)

    for copy in started:
        copy.wait_send()
    for h in range(HEADS):
        store_head(h).wait()
    pltpu.make_async_remote_copy(
        src_ref=req_send.at[pl.ds(0, CTX - 1)],
        dst_ref=req_recv.at[pl.ds(0, CTX - 1)],
        send_sem=req_sem.at[0],
        recv_sem=req_sem.at[1],
        device_id={"ctx": me},
    ).wait_send()
    for t in range(TILES):
        pltpu.make_async_remote_copy(
            src_ref=pack_send.at[t, pl.ds(0, (CTX - 1) * 16), :],
            dst_ref=pack_recv.at[t, pl.ds(0, (CTX - 1) * 16), :],
            send_sem=pack_ssem.at[t],
            recv_sem=pack_rsem.at[t],
            device_id={"ctx": me},
        ).wait_send()


def on_device(latent_cache, queries, chosen, key_up, value_up):
    any_spec = pl.BlockSpec(memory_space=pl.ANY)
    return pl.pallas_call(
        kernel,
        out_shape=jax.ShapeDtypeStruct((ROWS, HEADS * 128), BF),
        in_specs=[any_spec] * 5,
        out_specs=any_spec,
        scratch_shapes=[
            pltpu.VMEM((BD, SHARE), BF),
            pltpu.VMEM((ROWS, HEADS * 192), BF),
            pltpu.VMEM((32, ROWS), jnp.int32),
            pltpu.VMEM((HEADS, 128, 512), BF),
            pltpu.VMEM((HEADS, 512, 128), BF),
            pltpu.VMEM((CTX, 1, 128), F32),
            pltpu.VMEM((CTX, 1, 128), F32),
            pltpu.VMEM((TILES, CTX * 16, 128), BF),
            pltpu.VMEM((TILES, CTX * 16, 128), BF),
            pltpu.VMEM((8, 8, SLOTS, 640), BF),
            pltpu.VMEM((KEYS, 128), BF),
            pltpu.VMEM((HEADS, ROWS, 768), BF),
            pltpu.VMEM((HEADS, ROWS, 512), F32),
            pltpu.VMEM((HEADS, ROWS, 128), F32),
            pltpu.VMEM((HEADS, ROWS, 128), F32),
            pltpu.VMEM((ROWS, HEADS * 128), BF),
            pltpu.SemaphoreType.DMA((5,)),
            pltpu.SemaphoreType.DMA((2,)),
            pltpu.SemaphoreType.DMA((TILES,)),
            pltpu.SemaphoreType.DMA((TILES,)),
            pltpu.SemaphoreType.DMA((8, 7)),
            pltpu.SemaphoreType.DMA((8, 7)),
            pltpu.SemaphoreType.DMA((HEADS,)),
        ],
        compiler_params=pltpu.CompilerParams(
            collective_id=0, has_side_effects=True, vmem_limit_bytes=56 * 1024 * 1024
        ),
        cost_estimate=pl.CostEstimate(
            flops=15_000_000_000, bytes_accessed=8_000_000, transcendentals=6_300_000
        ),
        name="sparse_latent_attention",
    )(latent_cache, queries, chosen.T, key_up, value_up)


def solution(mesh):
    return jax.shard_map(
        on_device,
        mesh=mesh,
        in_specs=(
            P("ctx", None),
            P("ctx", "head"),
            P("ctx", None),
            P("head", None, None),
            P("head", None, None),
        ),
        out_specs=P("ctx", "head"),
        check_vma=False,
    )
```

```python
import functools

import jax
import jax.numpy as jnp
from jax import lax
from jax.experimental import pallas as pl
from jax.experimental.pallas import tpu as pltpu
from jax.sharding import PartitionSpec as P

BF = jnp.bfloat16
F32 = jnp.float32
CTX = 32
HEADS = 16
ROWS = 128
BD = 64
CAP = 3
POOL = 44
SLOTS = 48
SHARE = 4608
KEYS = 8 * SLOTS
CHUNKS = ((0, 1), (2, 3), (4,), (5, 6), (7,))
TILES = 7
AHEAD = 3
HP = 8
HIDE = -1e30
SCALE = (192**-0.5) * 1.4426950408889634


def nn(a, b):
    return lax.dot_general(a, b, (((1,), (0,)), ((), ())), preferred_element_type=F32)


def nt(a, b):
    return lax.dot_general(a, b, (((1,), (1,)), ((), ())), preferred_element_type=F32)


def iota(shape, dim):
    return lax.broadcasted_iota(jnp.int32, shape, dim)


def ones(cond):
    return jnp.where(cond, 1.0, 0.0).astype(BF)


def slot_of_row(r):
    return jnp.where(r < 5, 0, jnp.where(r < 10, 1, 2))


def kernel(
    cache_hbm, queries_hbm, chosen_hbm, kup_hbm, vup_hbm, out_hbm,
    shard, qraw, picks, kup, vup, req_send, req_recv, pack_send, pack_recv,
    pool, slot_oh, qext, acc, top, total, result,
    in_sem, req_sem, pack_ssem, pack_rsem, gat_ssem, gat_rsem, out_sem,
):
    me = lax.axis_index("ctx")
    hd = lax.axis_index("head")
    core = lax.rem(hd, 2)
    up = lax.rem(hd + 2, 8)
    down = lax.rem(hd + 6, 8)
    mate = hd + 1 - 2 * core
    far = lax.rem(hd + 4, 8)

    loads = []
    for n, (src, dst) in enumerate(
        (
            (chosen_hbm, picks),
            (cache_hbm.at[:, pl.ds(pl.multiple_of(hd * SHARE, 128), SHARE)], shard),
            (queries_hbm, qraw),
            (kup_hbm, kup),
            (vup_hbm, vup),
        )
    ):
        load = pltpu.make_async_copy(src, dst, in_sem.at[n])
        load.start()
        loads.append(load)

    barrier = pltpu.get_barrier_semaphore()

    def greet(k, carry):
        pl.semaphore_signal(barrier, inc=1, device_id={"ctx": lax.rem(me + k, CTX)})
        return carry

    lax.fori_loop(1, CTX, greet, 0)
    for peer in (up, down, far, mate):
        pl.semaphore_signal(barrier, inc=1, device_id={"head": peer})

    loads[0].wait()
    pick = picks[...]
    hi, lo = lax.shift_right_logical(pick, 6), pick & 63
    own_i = iota((CTX, ROWS), 0)
    blk_i = iota((128, ROWS), 0) & 63
    hi_oh = jnp.concatenate([ones(hi[j : j + 1] == own_i) for j in range(32)], axis=1)
    lo_oh = jnp.concatenate([ones(lo[j : j + 1] == blk_i) for j in range(32)], axis=1)
    flags = ones(nt(hi_oh, lo_oh) > 0.5)
    lane_r, lane_c = iota((128, 128), 0), iota((128, 128), 1)
    upto = ones((lane_r <= lane_c) & ((lane_r >> 6) == (lane_c >> 6)))
    rank = nn(flags, upto)
    hit = [(flags.astype(F32) > 0.5) & (rank == float(c + 1)) for c in range(CAP)]
    order = jnp.where(flags.astype(F32) > 0.5, rank, 0.0)
    for o in range(CTX):
        req_send[o] = order[o : o + 1]
    req_recv[me] = req_send[me]
    mine = pl.ds(pl.multiple_of(me * 16, 16), 16)

    pl.semaphore_wait(barrier, CTX - 1 + 4)

    def ask(k, carry):
        to = lax.rem(me + k, CTX)
        pltpu.make_async_remote_copy(
            src_ref=req_send.at[to],
            dst_ref=req_recv.at[me],
            send_sem=req_sem.at[0],
            recv_sem=req_sem.at[1],
            device_id={"ctx": to},
        ).start()
        return carry

    lax.fori_loop(1, CTX, ask, 0)

    n_lane = nt(jnp.ones((8, 128), BF), flags) * 0.5
    wide_o, wide_l = iota((CTX, CTX * 16), 0), iota((CTX, CTX * 16), 1) >> 4
    count = nn(n_lane.astype(BF), ones(wide_o == wide_l))[:1]
    base = nn(n_lane.astype(BF), ones(wide_o < wide_l))[:1]
    row_l = iota((1, CTX * 16), 1) & 15
    slot_s = iota((SLOTS, CTX * 16), 0).astype(F32)

    def place(c, rows):
        return ones(jnp.where(rows & (c < count), base + c, -1.0) == slot_s)

    c_row = slot_of_row(row_l)
    part = row_l - 5 * c_row
    spread = jnp.concatenate(
        [place(c_row.astype(F32), (row_l < 15) & (part == i)) for i in range(5)], axis=0
    )
    rest = [place(float(c), row_l == 15) for c in range(CAP)]

    n_row = n_lane[:1]
    base_row = nn(n_lane.astype(BF), ones(iota((CTX, CTX), 0) < iota((CTX, CTX), 1)))[:1]
    lane_v = iota((8, 128), 1)
    block_v = jnp.where(lane_v < 64, lane_v, 0).astype(F32).astype(BF)
    slot_c = iota((SLOTS, CTX), 0).astype(F32)
    owner_v = iota((1, CTX), 1).astype(F32) * 64.0
    ids = jnp.zeros((SLOTS, CTX), F32)
    for c in range(CAP):
        ident = owner_v + nt(block_v, ones(hit[c]))[:1]
        at = jnp.where(float(c) < n_row, base_row + float(c), -1.0) == slot_c
        ids = ids + jnp.where(at, ident, 0.0)
    ids = jnp.broadcast_to(jnp.sum(ids, axis=1, keepdims=True), (SLOTS, ROWS))
    pick_f = pick.astype(F32)
    found = jnp.zeros((SLOTS, ROWS), F32)
    for j in range(32):
        found = jnp.where(pick_f[j : j + 1] == ids, 1.0, found)
    hidden = jnp.where((found < 0.5) | (iota((SLOTS, ROWS), 0) >= POOL), HIDE, 0.0)
    hide = jnp.concatenate([hidden, jnp.zeros((ROWS - SLOTS, ROWS), F32)], axis=0).T.astype(BF)

    loads[2].wait()
    loads[3].wait()
    lane_q = iota((ROWS, 128), 1)
    for pair in range(HEADS // 2):
        a, b, c = [
            qraw[:, (3 * pair + i) * 128 : (3 * pair + i + 1) * 128].astype(F32) for i in range(3)
        ]
        b_r, c_r = pltpu.roll(b, 64, 1), pltpu.roll(c, 64, 1)
        halves = (
            (a, jnp.where(lane_q < 64, b, b_r)),
            (jnp.where(lane_q < 64, b_r, c_r), jnp.where(lane_q < 64, c_r, c)),
        )
        for k, (nope, rope) in enumerate(halves):
            h = 2 * pair + k
            qext[h, :, :512] = nn(nope.astype(BF), kup[h]).astype(BF)
            qext[h, :, 512:640] = rope.astype(BF)
            qext[h, :, 640:] = hide
    slot_oh[...] = ones(iota((8, SLOTS, 128), 1) == iota((8, SLOTS, 128), 2)).reshape(KEYS, 128)

    loads[1].wait()
    pltpu.make_async_remote_copy(
        src_ref=req_send.at[pl.ds(0, CTX - 1)],
        dst_ref=req_recv.at[pl.ds(0, CTX - 1)],
        send_sem=req_sem.at[0],
        recv_sem=req_sem.at[1],
        device_id={"ctx": me},
    ).wait_recv()
    rep = ones((iota((CTX * 16, CTX), 0) >> 4) == iota((CTX * 16, CTX), 1))
    got = nn(rep, req_recv[:, 0, :].astype(BF))
    row = iota((CTX * 16, 128), 0) & 15
    lane = iota((CTX * 16, 128), 1)
    c_of = slot_of_row(row)
    asked = (got == (c_of + 1).astype(F32)) & (row < 15)
    sel = [ones(asked & (row - 5 * c_of == 2 * k + (lane >> 6))) for k in range(3)]
    spare = [ones((row == 15) & (lane >= 64) & (got == float(c + 1))) for c in range(CAP)]

    def tile(u):
        return shard[:, u * 128 : u * 128 + 128]

    def give(t):
        def one(k, carry):
            to = lax.rem(me + k, CTX)
            pltpu.make_async_remote_copy(
                src_ref=pack_send.at[t, pl.ds(pl.multiple_of(to * 16, 16), 16), :],
                dst_ref=pack_recv.at[t, mine, :],
                send_sem=pack_ssem.at[t],
                recv_sem=pack_rsem.at[t],
                device_id={"ctx": to},
            ).start()
            return carry

        lax.fori_loop(1, CTX, one, 0)

    for t in range(TILES):
        if t < 6:
            last = sel[2] + spare[t % 3]
            src = [tile(5 * t + i) for i in range(5)] + [tile(30 + t // 3)]
        else:
            last = sel[2]
            src = [tile(min(32 + i, 35)) for i in range(6)]
        packed = nn(jnp.concatenate(sel[:2] + [last], axis=1), jnp.concatenate(src, axis=0))
        pack_send[t] = packed.astype(BF)
        pack_recv[t, mine, :] = pack_send[t, mine, :]
        if t < AHEAD:
            give(t)

    def gather_copy(p, kind, piece, to):
        part = pool.at[p, piece]
        return pltpu.make_async_remote_copy(
            src_ref=part,
            dst_ref=part,
            send_sem=gat_ssem.at[p, kind],
            recv_sem=gat_rsem.at[p, kind],
            device_id={"head": to},
        )

    started = []

    def send(p, kind, piece, to):
        copy = gather_copy(p, kind, piece, to)
        copy.start()
        started.append(copy)

    tiles = {}
    lane48 = iota((SLOTS, 128), 1)

    def share(p):
        u = 9 * (p // 2)
        if p % 2 == 0:
            cols = [tiles[u + k] for k in range(4)]
            cols.append(jnp.where(lane48 < 64, tiles[u + 4], 0.0))
        else:
            r = [pltpu.roll(tiles[u + k], 64, 1) for k in range(4, 9)]
            cols = [jnp.where(lane48 < 64, r[k], r[k + 1]) for k in range(4)]
            cols.append(jnp.where(lane48 < 64, 0.0, tiles[u + 8]))
        pool[p, hd] = jnp.concatenate(cols, axis=1).astype(BF)
        send(p, 0, hd, up)
        send(p, 1, hd, down)
        send(p, 2, hd, far)
        send(p, 3, hd, mate)

    def arrive(t):
        pltpu.make_async_remote_copy(
            src_ref=pack_send.at[t, pl.ds(0, (CTX - 1) * 16), :],
            dst_ref=pack_recv.at[t, pl.ds(0, (CTX - 1) * 16), :],
            send_sem=pack_ssem.at[t],
            recv_sem=pack_rsem.at[t],
            device_id={"ctx": me},
        ).wait_recv()
        if t + AHEAD < TILES:
            give(t + AHEAD)
        moved = nn(spread, pack_recv[t])
        for i in range(5):
            tiles[5 * t + i if t < 6 else 32 + i] = moved[SLOTS * i : SLOTS * i + SLOTS]
        if t == 5:
            for k in range(2):
                tiles[30 + k] = sum(nn(rest[c], pack_recv[3 * k + c]) for c in range(CAP))
        for p in ((0,), (1,), (2,), (3,), (4,), (5, 6), (7,))[t]:
            share(p)

    def relay(p):
        for kind, piece in ((0, down), (1, up), (2, far)):
            gather_copy(p, kind, piece, piece).wait_recv()
            send(p, 4 + kind, piece, mate)

    def ready(j):
        for p in CHUNKS[j]:
            for kind in (3, 4, 5, 6):
                gather_copy(p, kind, mate, mate).wait_recv()

    def store_head(h):
        lanes = pl.ds(h * 128, 128)
        return pltpu.make_async_copy(result.at[:, lanes], out_hbm.at[:, lanes], out_sem.at[h])

    rows_step = HP * ROWS

    def attend(j, n):
        hs = pl.ds(n * HP, HP)
        wide = len(CHUNKS[j]) * KEYS // 128
        held = [pool[p].reshape(KEYS, 640) for p in CHUNKS[j]]
        whole = jnp.concatenate(
            [jnp.concatenate([x, slot_oh[...]], axis=1) for x in held], axis=0
        )
        keys = jnp.concatenate([x[:, :512] for x in held], axis=0)
        q = qext[hs].reshape(rows_step, 768)
        s = nt(q, whole)
        m_new = jnp.broadcast_to(jnp.max(s, axis=1, keepdims=True), (rows_step, 128))
        if j > 0:
            m_old = top[hs].reshape(rows_step, 128)
            m_new = jnp.maximum(m_new, m_old)
        e = jnp.exp2((s - jnp.concatenate([m_new] * wide, axis=1)) * SCALE)
        part_sum = sum(e[:, 128 * k : 128 * k + 128] for k in range(wide))
        o = nn(e.astype(BF), keys)
        if j > 0:
            alpha = jnp.exp2((m_old - m_new) * SCALE)
            part_sum = part_sum + total[hs].reshape(rows_step, 128) * alpha
            o = o + acc[hs].reshape(rows_step, 512) * jnp.concatenate([alpha] * 4, axis=1)
        if j < len(CHUNKS) - 1:
            top[hs] = m_new.reshape(HP, ROWS, 128)
            total[hs] = part_sum.reshape(HP, ROWS, 128)
            acc[hs] = o.reshape(HP, ROWS, 512)
        else:
            mixed = (o * (1.0 / jnp.sum(part_sum, axis=1, keepdims=True))).astype(BF)
            for k in range(HP):
                h = n * HP + k
                result[:, h * 128 : h * 128 + 128] = nn(
                    mixed[k * ROWS : (k + 1) * ROWS], vup[h]
                ).astype(BF)
                store_head(h).start()

    arrive(0)
    arrive(1)
    relay(0)
    arrive(2)
    relay(1)
    arrive(3)
    ready(0)
    attend(0, 0)
    relay(2)
    arrive(4)
    attend(0, 1)
    relay(3)
    arrive(5)
    ready(1)
    attend(1, 0)
    relay(4)
    arrive(6)
    attend(1, 1)
    relay(5)
    ready(2)
    attend(2, 0)
    relay(6)
    attend(2, 1)
    relay(7)
    ready(3)
    attend(3, 0)
    attend(3, 1)
    ready(4)
    loads[4].wait()
    attend(4, 0)
    attend(4, 1)

    for copy in started:
        copy.wait_send()
    for h in range(HEADS):
        store_head(h).wait()
    pltpu.make_async_remote_copy(
        src_ref=req_send.at[pl.ds(0, CTX - 1)],
        dst_ref=req_recv.at[pl.ds(0, CTX - 1)],
        send_sem=req_sem.at[0],
        recv_sem=req_sem.at[1],
        device_id={"ctx": me},
    ).wait_send()
    for t in range(TILES):
        pltpu.make_async_remote_copy(
            src_ref=pack_send.at[t, pl.ds(0, (CTX - 1) * 16), :],
            dst_ref=pack_recv.at[t, pl.ds(0, (CTX - 1) * 16), :],
            send_sem=pack_ssem.at[t],
            recv_sem=pack_rsem.at[t],
            device_id={"ctx": me},
        ).wait_send()


def on_device(latent_cache, queries, chosen, key_up, value_up):
    any_spec = pl.BlockSpec(memory_space=pl.ANY)
    return pl.pallas_call(
        kernel,
        out_shape=jax.ShapeDtypeStruct((ROWS, HEADS * 128), BF),
        in_specs=[any_spec] * 5,
        out_specs=any_spec,
        scratch_shapes=[
            pltpu.VMEM((BD, SHARE), BF),
            pltpu.VMEM((ROWS, HEADS * 192), BF),
            pltpu.VMEM((32, ROWS), jnp.int32),
            pltpu.VMEM((HEADS, 128, 512), BF),
            pltpu.VMEM((HEADS, 512, 128), BF),
            pltpu.VMEM((CTX, 1, 128), F32),
            pltpu.VMEM((CTX, 1, 128), F32),
            pltpu.VMEM((TILES, CTX * 16, 128), BF),
            pltpu.VMEM((TILES, CTX * 16, 128), BF),
            pltpu.VMEM((8, 8, SLOTS, 640), BF),
            pltpu.VMEM((KEYS, 128), BF),
            pltpu.VMEM((HEADS, ROWS, 768), BF),
            pltpu.VMEM((HEADS, ROWS, 512), F32),
            pltpu.VMEM((HEADS, ROWS, 128), F32),
            pltpu.VMEM((HEADS, ROWS, 128), F32),
            pltpu.VMEM((ROWS, HEADS * 128), BF),
            pltpu.SemaphoreType.DMA((5,)),
            pltpu.SemaphoreType.DMA((2,)),
            pltpu.SemaphoreType.DMA((TILES,)),
            pltpu.SemaphoreType.DMA((TILES,)),
            pltpu.SemaphoreType.DMA((8, 7)),
            pltpu.SemaphoreType.DMA((8, 7)),
            pltpu.SemaphoreType.DMA((HEADS,)),
        ],
        compiler_params=pltpu.CompilerParams(
            collective_id=0, has_side_effects=True, vmem_limit_bytes=56 * 1024 * 1024
        ),
        cost_estimate=pl.CostEstimate(
            flops=15_000_000_000, bytes_accessed=8_000_000, transcendentals=6_300_000
        ),
        name="sparse_latent_attention",
    )(latent_cache, queries, chosen.T, key_up, value_up)


def solution(mesh):
    return jax.shard_map(
        on_device,
        mesh=mesh,
        in_specs=(
            P("ctx", None),
            P("ctx", "head"),
            P("ctx", None),
            P("head", None, None),
            P("head", None, None),
        ),
        out_specs=P("ctx", "head"),
        check_vma=False,
    )
```
